32 devices in a mesh: leaf: 16 (over z, y, x), rhs: 2 (over core).
Axes of the slice: x: 2, y: 2, z: 4, core: 2. Of those that a mesh axis runs over, the one named last changes fastest.
Arguments:
- leaf_skel: bfloat16 [2, 16, 128, 512], P(None, 'leaf', 'rhs'), may hold values from -6 to 6
- ranks: int32 [2, 16, 5], P(None, 'leaf'), may hold values from 64 to 256, as said below
- up_weight: bfloat16 [2, 15360, 512], P(None, 'leaf', 'rhs'), may hold values from -0.1875 to 0.1875
- down_weight: bfloat16 [2, 31232, 512], P(None, 'leaf', 'rhs'), may hold values from -1 to 1
Outputs:
- leaf_result: bfloat16 [2, 16, 128, 512], P(None, 'leaf', 'rhs')
The draws below stay inside these ranges and needn't reach their ends.
Inputs may be any that keep to these rules, and one draw needn't show every extreme that they name: ranks[b, i, l] is the rank of the level-l node above leaf i of tree b: equal for all leaves under one node; some node reaches 256.
All inputs are finite; a program needn't handle non-finite values.
Results may differ from the reference program's by a relative error of at most 0.022.
Values may be sent and summed in bfloat16 or wider, within the bound.
A program may use at most 64 MiB of HBM per device.

```python
import jax
import jax.numpy as jnp

K = 256
SK = 512
BOX = 2
LEV = 4
RHS = 128
RUP = 960
RDN = 1952
N_LEAF = 16


def draw_ranks(key, part):
    key = jax.random.fold_in(key, 7)
    spread = 3 * K // 4
    base = jax.random.randint(key, (BOX, LEV + 1, N_LEAF), 0, spread + 1)
    leaves = jnp.arange(N_LEAF)
    owners = leaves[None, :] // (2 ** jnp.arange(LEV + 1))[:, None]
    picked = jnp.take_along_axis(base, jnp.broadcast_to(owners[None], base.shape), axis=2)
    value = K // 4 + picked * picked // spread
    first = (owners == 0)[None] & (jnp.arange(BOX) == 0)[:, None, None]
    value = jnp.where(first, K, value)
    return jnp.transpose(value, (0, 2, 1)).astype(jnp.int32)


def draw_down_weight(key, part):
    key = jax.random.fold_in(key, 11)
    width_all = 2 * K
    root_rows = width_all // 2 ** LEV
    row_ids = jnp.arange(RDN)
    scales = jnp.full((RDN,), (1.0 / width_all) ** 0.5, jnp.float32)
    for level in range(LEV):
        width = width_all >> level
        start = root_rows + 2 * (2 * width_all - (2 * width_all >> level))
        own_rows = (row_ids >= start) & (row_ids < start + width)
        parent_rows = (row_ids >= start + width) & (row_ids < start + 2 * width)
        scales = jnp.where(own_rows, (0.4 / (2 * width_all)) ** 0.5, scales)
        scales = jnp.where(parent_rows, (1.6 / (2 * width_all)) ** 0.5, scales)
    noise = jnp.clip(jax.random.normal(key, (BOX, N_LEAF, RDN, width_all), jnp.float32), -6.0, 6.0)
    value = noise * scales[None, None, :, None]
    return value.reshape(BOX, N_LEAF * RDN, width_all).astype(jnp.bfloat16)


def level_of(key, shape, split, smallest, largest):
    def one(position, shards_of):
        draws = jax.random.uniform(jax.random.fold_in(jax.random.fold_in(key, 6), position), (shards_of,), jnp.float32, smallest / len(split), largest / len(split))
        return jnp.repeat(jnp.exp(draws), shape[position] // shards_of).reshape((-1,) + (1,) * (len(shape) - position - 1))

    factor_of = one(*split[0])
    for cut in split[1:]:
        factor_of = factor_of * one(*cut)
    return factor_of


def scatter_about(stream_key, shape, deviation, most, split=(), held_as=jnp.bfloat16):
    gain = level_of(stream_key, shape, split, -0.22, 0.18) if split else 1.0
    values = jax.random.normal(stream_key, shape, jnp.float32) * deviation * gain
    return jnp.minimum(jnp.maximum(values, -most), most).astype(held_as)


def setup_inputs(seed: int = 0) -> dict:
    arg_keys = jax.random.split(jax.random.key(seed), 5)
    leaf_skel = scatter_about(arg_keys[0], (BOX, N_LEAF, RHS, SK), 1.0, 6.0, ((1, 16), (2, 2)))
    ranks = draw_ranks(jax.random.fold_in(arg_keys[4], 71), 0)
    up_weight = scatter_about(arg_keys[2], (BOX, N_LEAF * RUP, SK), (2 * SK) ** -0.5, 0.1875, ((1, 16), (2, 2)))
    down_weight = draw_down_weight(jax.random.fold_in(arg_keys[4], 71), 0)
    return {"leaf_skel": leaf_skel, "ranks": ranks, "up_weight": up_weight, "down_weight": down_weight}


def column_keep(rank_table, width):
    column_ids = jnp.arange(width) % (width // 2)
    return column_ids[None, None, None, :] < rank_table[:, :, None, None]


def reference(leaf_skel, ranks, up_weight, down_weight):
    width_all = 2 * K
    levels = ranks.shape[-1] - 1
    up_rows = up_weight.reshape(BOX, N_LEAF, RUP, width_all)
    down_rows = down_weight.reshape(BOX, N_LEAF, RDN, width_all)
    current = jnp.where(column_keep(ranks[:, :, 0], width_all), leaf_skel, 0.0).astype(jnp.bfloat16)
    saved = [current]
    for level in range(levels):
        width = width_all >> level
        offset = 2 * width_all - (2 * width_all >> level)
        nodes = N_LEAF >> (level + 1)
        matrix = up_rows[:, :, offset:offset + width].reshape(BOX, nodes, 2 * width_all, width_all).astype(jnp.float32)
        pairs = current.reshape(BOX, nodes, 2, RHS, width_all).transpose(0, 1, 3, 2, 4)
        pairs = pairs.reshape(BOX, nodes, RHS, 2 * width_all).astype(jnp.float32)
        parent = jnp.einsum("bnrk,bnkm->bnrm", pairs, matrix)
        rank_now = ranks[:, ::(1 << (level + 1)), level + 1]
        current = jnp.where(column_keep(rank_now, width_all), parent, 0.0).astype(jnp.bfloat16)
        saved.append(current)
    width = width_all >> levels
    nodes = N_LEAF >> levels
    matrix = down_rows[:, :, :width].reshape(BOX, nodes, width_all, width_all).astype(jnp.float32)
    value = jnp.einsum("bnrk,bnkm->bnrm", saved[levels].astype(jnp.float32), matrix)
    result = jnp.where(column_keep(ranks[:, ::(1 << levels), levels], width_all), value, 0.0).astype(jnp.bfloat16)
    for level in reversed(range(levels)):
        width = width_all >> level
        offset = (width_all >> levels) + 2 * (2 * width_all - (2 * width_all >> level))
        nodes = N_LEAF >> level
        block = down_rows[:, :, offset:offset + 2 * width].reshape(BOX, N_LEAF, 2, width, width_all)
        g_part = block[:, :, 0].reshape(BOX, nodes, width_all, width_all)
        h_part = block[:, :, 1].reshape(BOX, nodes, width_all, width_all)
        matrix = jnp.concatenate([g_part, h_part], axis=2).astype(jnp.float32)
        parent_rep = jnp.repeat(result, 2, axis=1)
        acting = jnp.concatenate([saved[level], parent_rep], axis=3).astype(jnp.float32)
        value = jnp.einsum("bnrk,bnkm->bnrm", acting, matrix)
        result = jnp.where(column_keep(ranks[:, ::(1 << level), level], width_all), value, 0.0).astype(jnp.bfloat16)
    return result
```

```python
import functools

import jax
import jax.numpy as jnp
from jax import lax
from jax.experimental import pallas as pl
from jax.experimental.pallas import tpu as pltpu
from jax.sharding import PartitionSpec as P

MESH = pl.DeviceIdType.MESH
UNROLL = 16


def folds_of(width):
    return 1 if width >= 128 else min(128 // width, 4)


def make_phases(levels, width_all):
    phases = []
    for level in range(levels):
        group = 2 << level
        phases.append((group, group, width_all // group))
    for level in range(levels, 0, -1):
        group = 1 << level
        phases.append((group, group // 2, width_all // (group // 2)))
    return phases


def make_chunks(levels, width_all, up_rows, down_rows):
    ups = [(2 * width_all - (2 * width_all >> l), width_all >> l) for l in range(levels)]
    root = width_all >> levels
    downs = [
        (root + 2 * (2 * width_all - (2 * width_all >> l)), 2 * (width_all >> l))
        for l in range(levels)
    ]
    fine = all(o % 16 == 0 and w % 16 == 0 for o, w in ups + downs + [(0, root)])
    if not fine:
        chunks = [(False, None, 0, up_rows), (True, None, 0, down_rows)]
        return chunks, [[0]] * levels, [1], [[1]] * levels
    chunks = [(False, 0) + ups[0], (False, 1) + ups[0]]
    up_at = [[0, 1]]
    for l in range(1, levels):
        up_at.append([len(chunks)])
        chunks.append((False, None) + ups[l])
    root_at = [len(chunks)]
    chunks.append((True, None, 0, root))
    down_at = [None] * levels
    for l in reversed(range(levels)):
        down_at[l] = [len(chunks)]
        chunks.append((True, None) + downs[l])
    return chunks, up_at, root_at, down_at


def kernel(dims, skel_hbm, ranks, up_hbm, down_hbm, out, *scratch):
    levels, width_all, boxes, rhs, n_leaf, up_rows, down_rows = dims
    phases = make_phases(levels, width_all)
    chunks, up_at, root_at, down_at = make_chunks(levels, width_all, up_rows, down_rows)
    count = len(phases)
    skel, up, down, own_sum = scratch[:4]
    sends = scratch[4 : 4 + count]
    recvs = scratch[4 + count : 4 + 2 * count]
    skel_sem, local_sem, w_send, w_recv, p_send, p_recv = scratch[4 + 2 * count :]

    leaf = lax.axis_index("leaf")
    core = lax.axis_index("rhs")
    other = 1 - core
    span = 1 << levels
    span_base = leaf - leaf % span

    barrier = pltpu.get_barrier_semaphore()
    pl.semaphore_signal(barrier, inc=1, device_id=(leaf, other), device_id_type=MESH)

    def greet(d):
        target = span_base + (leaf + d) % span
        pl.semaphore_signal(barrier, inc=1, device_id=(target, core), device_id_type=MESH)

    if span <= UNROLL:
        for d in range(1, span):
            greet(d)
    else:
        pl.loop(1, span)(greet)

    def box_rows(chunk):
        is_down, box, first, rows = chunk
        boxes_of = slice(None) if box is None else pl.ds(box, 1)
        source = (down_hbm if is_down else up_hbm).at[boxes_of, pl.ds(first, rows), :]
        target = (down if is_down else up).at[core, boxes_of, pl.ds(first, rows), :]
        return source, target

    def arriving(chunk):
        is_down, box, first, rows = chunk
        boxes_of = slice(None) if box is None else pl.ds(box, 1)
        return (down if is_down else up).at[other, boxes_of, pl.ds(first, rows), :]

    skel_copy = pltpu.make_async_copy(skel_hbm, skel, skel_sem)
    skel_copy.start()
    local = []
    for i, chunk in enumerate(chunks):
        source, target = box_rows(chunk)
        copy = pltpu.make_async_copy(source, target, local_sem.at[i])
        copy.start()
        local.append(copy)

    pl.semaphore_wait(barrier, span)

    remote = []
    for i, chunk in enumerate(chunks):
        source, target = box_rows(chunk)
        copy = pltpu.make_async_remote_copy(
            src_ref=source,
            dst_ref=target,
            send_sem=w_send.at[i],
            recv_sem=w_recv.at[i],
            device_id=(leaf, other),
            device_id_type=MESH,
        )
        copy.start()
        remote.append(copy)

    ready = set()

    def need(indices, box):
        for i in indices:
            if i in ready or chunks[i][1] not in (None, box):
                continue
            ready.add(i)
            local[i].wait()
            landed = arriving(chunks[i])
            pltpu.make_async_copy(landed, landed, w_recv.at[i]).wait()

    def times(block, weights, box, first, rows):
        return jnp.concatenate(
            [
                jnp.dot(
                    block,
                    weights[half, box, first : first + rows, :],
                    preferred_element_type=jnp.float32,
                )
                for half in range(2)
            ],
            axis=1,
        )

    def send(phase, box, value):
        group, slices, width = phases[phase]
        member = leaf % group
        base = leaf - member
        folds = folds_of(width)
        rows = rhs // folds
        value = value.astype(jnp.bfloat16)
        for k in range(slices):
            piece = value[:, k * width : (k + 1) * width]
            if folds > 1:
                piece = jnp.concatenate(
                    [piece[f * rows : (f + 1) * rows] for f in range(folds)], axis=1
                )
            sends[phase][box, k] = piece

        def one(d):
            there = (member + d) % group
            pltpu.make_async_remote_copy(
                src_ref=sends[phase].at[box, there % slices],
                dst_ref=recvs[phase].at[box, d - 1],
                send_sem=p_send.at[phase, box],
                recv_sem=p_recv.at[phase, box],
                device_id=(base + there, core),
                device_id_type=MESH,
            ).start()

        if group <= UNROLL:
            for d in range(1, group):
                one(d)
        else:
            pl.loop(1, group)(one)

    def keep(value, rank, first_column, width):
        columns = lax.broadcasted_iota(jnp.int32, value.shape, 1) % width + first_column
        return jnp.where(columns % (width_all // 2) < rank, value, 0.0)

    def receive(phase, box, level):
        group, slices, width = phases[phase]
        mine = leaf % slices
        folds = folds_of(width)
        rows = rhs // folds
        landed = recvs[phase].at[box]
        pltpu.make_async_copy(landed, landed, p_recv.at[phase, box]).wait()
        total = sends[phase][box, mine].astype(jnp.float32)
        if group <= UNROLL:
            for d in range(group - 1):
                total = total + recvs[phase][box, d].astype(jnp.float32)
        else:
            total = total + jnp.sum(recvs[phase][box].astype(jnp.float32), axis=0)
        total = keep(total, ranks[box, 0, level], mine * width, width)
        if folds > 1:
            total = jnp.concatenate(
                [total[:, f * width : (f + 1) * width] for f in range(folds)], axis=0
            )
        return total.astype(jnp.bfloat16)

    def down_first(level):
        return (width_all >> levels) + 2 * (2 * width_all - (2 * width_all >> level))

    saved = [[None] * boxes for _ in range(levels + 1)]

    def own_terms(level):
        width = width_all >> level
        for box in range(boxes):
            need(down_at[level], box)
            own_sum[level, box] = times(saved[level][box], down, box, down_first(level), width)

    skel_copy.wait()
    for level in range(levels):
        width = width_all >> level
        offset = 2 * width_all - (2 * width_all >> level)
        for box in range(boxes):
            if level == 0:
                block = keep(
                    skel[box, 0].astype(jnp.float32), ranks[box, 0, 0], 0, width_all
                ).astype(jnp.bfloat16)
            else:
                block = receive(level - 1, box, level)
            saved[level][box] = block
            need(up_at[level], box)
            send(level, box, times(block, up, box, offset, width))
        if level == levels - 1:
            own_terms(level)
            if level - 1 > 1:
                own_terms(level - 1)
    phase = levels
    for box in range(boxes):
        block = receive(levels - 1, box, levels)
        need(root_at, box)
        send(phase, box, times(block, down, box, 0, width_all >> levels))
    for level in reversed(range(levels - 2 if levels - 2 > 1 else levels - 1)):
        own_terms(level)
    for level in reversed(range(levels)):
        width = width_all >> level
        for box in range(boxes):
            block = receive(phase, box, level + 1)
            value = own_sum[level, box] + times(
                block, down, box, down_first(level) + width, width
            )
            if level:
                send(phase + 1, box, value)
            else:
                out[box, 0] = keep(value, ranks[box, 0, 0], 0, width_all).astype(out.dtype)
        phase += 1

    for copy in remote:
        copy.wait_send()
    for p, (group, slices, width) in enumerate(phases):
        for box in range(boxes):
            sent = recvs[p].at[box]
            pltpu.make_async_copy(sent, sent, p_send.at[p, box]).wait()


def per_device(dims, leaf_skel, ranks, up_weight, down_weight):
    levels, width_all, boxes, rhs, n_leaf, up_rows, down_rows = dims
    phases = make_phases(levels, width_all)
    chunks = make_chunks(levels, width_all, up_rows, down_rows)[0]
    half = up_weight.shape[-1]

    def piece(width):
        folds = folds_of(width)
        return rhs // folds, folds * width

    sends = [pltpu.VMEM((boxes, s) + piece(w), jnp.bfloat16) for g, s, w in phases]
    recvs = [pltpu.VMEM((boxes, g - 1) + piece(w), jnp.bfloat16) for g, s, w in phases]
    dma = pltpu.SemaphoreType.DMA
    return pl.pallas_call(
        functools.partial(kernel, dims),
        out_shape=jax.ShapeDtypeStruct(leaf_skel.shape, leaf_skel.dtype),
        in_specs=[
            pl.BlockSpec(memory_space=pl.ANY),
            pl.BlockSpec(memory_space=pltpu.SMEM),
            pl.BlockSpec(memory_space=pl.ANY),
            pl.BlockSpec(memory_space=pl.ANY),
        ],
        out_specs=pl.BlockSpec(memory_space=pltpu.VMEM),
        scratch_shapes=[
            pltpu.VMEM(leaf_skel.shape, jnp.bfloat16),
            pltpu.VMEM((2, boxes, up_rows, half), jnp.bfloat16),
            pltpu.VMEM((2, boxes, down_rows, half), jnp.bfloat16),
            pltpu.VMEM((levels, boxes, rhs, width_all), jnp.float32),
        ]
        + sends
        + recvs
        + [
            dma,
            dma((len(chunks),)),
            dma((len(chunks),)),
            dma((len(chunks),)),
            dma((len(phases), boxes)),
            dma((len(phases), boxes)),
        ],
        compiler_params=pltpu.CompilerParams(
            collective_id=0, has_side_effects=True, vmem_limit_bytes=48 * 1024 * 1024
        ),
        cost_estimate=pl.CostEstimate(
            flops=4 * boxes * rhs * (up_rows + down_rows) * half * 2,
            bytes_accessed=4 * boxes * (up_rows + down_rows) * half,
            transcendentals=0,
        ),
    )(leaf_skel, ranks, up_weight, down_weight)


def solution(mesh):
    n_leaf, n_rhs = mesh.shape["leaf"], mesh.shape["rhs"]

    def whole(leaf_skel, ranks, up_weight, down_weight):
        dims = (
            ranks.shape[-1] - 1,
            leaf_skel.shape[-1],
            leaf_skel.shape[0],
            leaf_skel.shape[2] // n_rhs,
            n_leaf,
            up_weight.shape[1] // n_leaf,
            down_weight.shape[1] // n_leaf,
        )
        return jax.shard_map(
            functools.partial(per_device, dims),
            mesh=mesh,
            in_specs=(
                P(None, "leaf", "rhs", None),
                P(None, "leaf", None),
                P(None, "leaf", "rhs"),
                P(None, "leaf", "rhs"),
            ),
            out_specs=P(None, "leaf", "rhs", None),
            check_vma=False,
        )(leaf_skel, ranks, up_weight, down_weight)

    return whole
```

```python
import functools

import jax
import jax.numpy as jnp
from jax import lax
from jax.experimental import pallas as pl
from jax.experimental.pallas import tpu as pltpu
from jax.sharding import PartitionSpec as P

MESH = pl.DeviceIdType.MESH
UNROLL = 16


def folds_of(width):
    return 1 if width >= 128 else min(128 // width, 4)


def far_first(group):
    hops = [1, 1, 1, 2]
    count = lambda d: sum(h for bit, h in enumerate(hops) if d >> bit & 1)
    return sorted(range(1, group), key=count, reverse=True)


def make_phases(levels, width_all):
    phases = []
    for level in range(levels):
        group = 2 << level
        phases.append((group, group, width_all // group))
    for level in range(levels, 0, -1):
        group = 1 << level
        phases.append((group, group // 2, width_all // (group // 2)))
    return phases


def make_chunks(levels, width_all, up_rows, down_rows):
    ups = [(2 * width_all - (2 * width_all >> l), width_all >> l) for l in range(levels)]
    root = width_all >> levels
    downs = [
        (root + 2 * (2 * width_all - (2 * width_all >> l)), 2 * (width_all >> l))
        for l in range(levels)
    ]
    fine = all(o % 16 == 0 and w % 16 == 0 for o, w in ups + downs + [(0, root)])
    if not fine:
        chunks = [(False, None, 0, up_rows), (True, None, 0, down_rows)]
        return chunks, [[0]] * levels, [1], [[1]] * levels
    chunks = [(False, 0) + ups[0], (False, 1) + ups[0]]
    up_at = [[0, 1]]
    for l in range(1, levels):
        up_at.append([len(chunks)])
        chunks.append((False, None) + ups[l])
    root_at = [len(chunks)]
    chunks.append((True, None, 0, root))
    down_at = [None] * levels
    for l in reversed(range(levels)):
        down_at[l] = [len(chunks)]
        chunks.append((True, None) + downs[l])
    return chunks, up_at, root_at, down_at


def kernel(dims, skel_hbm, ranks_hbm, up_hbm, down_hbm, out, *scratch):
    levels, width_all, boxes, rhs, n_leaf, up_rows, down_rows = dims
    phases = make_phases(levels, width_all)
    chunks, up_at, root_at, down_at = make_chunks(levels, width_all, up_rows, down_rows)
    count = len(phases)
    skel, ranks, up, down, own_sum = scratch[:5]
    sends = scratch[5 : 5 + count]
    recvs = scratch[5 + count : 5 + 2 * count]
    skel_sem, ranks_sem, local_sem, w_send, w_recv, p_send, p_recv = scratch[5 + 2 * count :]

    leaf = lax.axis_index("leaf")
    core = lax.axis_index("rhs")
    other = 1 - core

    barrier = pltpu.get_barrier_semaphore()
    pl.semaphore_signal(barrier, inc=1, device_id=(leaf, other), device_id_type=MESH)

    for bit in range(levels):
        step = 1 << bit
        target = leaf + step * (1 - 2 * (leaf // step % 2))
        pl.semaphore_signal(barrier, inc=1, device_id=(target, core), device_id_type=MESH)

    def box_rows(chunk):
        is_down, box, first, rows = chunk
        boxes_of = slice(None) if box is None else pl.ds(box, 1)
        source = (down_hbm if is_down else up_hbm).at[boxes_of, pl.ds(first, rows), :]
        target = (down if is_down else up).at[core, boxes_of, pl.ds(first, rows), :]
        return source, target

    def arriving(chunk):
        is_down, box, first, rows = chunk
        boxes_of = slice(None) if box is None else pl.ds(box, 1)
        return (down if is_down else up).at[other, boxes_of, pl.ds(first, rows), :]

    skel_copy = pltpu.make_async_copy(skel_hbm, skel, skel_sem)
    skel_copy.start()
    ranks_copy = pltpu.make_async_copy(ranks_hbm, ranks, ranks_sem)
    ranks_copy.start()
    local = []
    for i, chunk in enumerate(chunks):
        source, target = box_rows(chunk)
        copy = pltpu.make_async_copy(source, target, local_sem.at[i])
        copy.start()
        local.append(copy)

    pl.semaphore_wait(barrier, levels + 1)

    remote = []
    for i, chunk in enumerate(chunks):
        source, target = box_rows(chunk)
        copy = pltpu.make_async_remote_copy(
            src_ref=source,
            dst_ref=target,
            send_sem=w_send.at[i],
            recv_sem=w_recv.at[i],
            device_id=(leaf, other),
            device_id_type=MESH,
        )
        copy.start()
        remote.append(copy)

    ready = set()

    def need(indices, box):
        for i in indices:
            if i in ready or chunks[i][1] not in (None, box):
                continue
            ready.add(i)
            local[i].wait()
            landed = arriving(chunks[i])
            pltpu.make_async_copy(landed, landed, w_recv.at[i]).wait()

    def times(block, weights, box, first, rows):
        return jnp.concatenate(
            [
                jnp.dot(
                    block,
                    weights[half, box, first : first + rows, :],
                    preferred_element_type=jnp.float32,
                )
                for half in range(2)
            ],
            axis=1,
        )

    def send(phase, box, value):
        group, slices, width = phases[phase]
        member = leaf % group
        base = leaf - member
        folds = folds_of(width)
        rows = rhs // folds
        value = value.astype(jnp.bfloat16)
        for k in range(slices):
            piece = value[:, k * width : (k + 1) * width]
            if folds > 1:
                piece = jnp.concatenate(
                    [piece[f * rows : (f + 1) * rows] for f in range(folds)], axis=1
                )
            sends[phase][box, k] = piece

        def one(d):
            there = member
            for bit in range(group.bit_length() - 1):
                step = 1 << bit
                there = there + step * (d // step % 2) * (1 - 2 * (member // step % 2))
            pltpu.make_async_remote_copy(
                src_ref=sends[phase].at[box, there % slices],
                dst_ref=recvs[phase].at[box, d - 1],
                send_sem=p_send.at[phase, box],
                recv_sem=p_recv.at[phase, box],
                device_id=(base + there, core),
                device_id_type=MESH,
            ).start()

        if group <= UNROLL:
            for d in far_first(group):
                one(d)
        else:
            pl.loop(1, group)(one)

    def keep(value, rank, first_column, width):
        columns = lax.broadcasted_iota(jnp.int32, value.shape, 1) % width + first_column
        return jnp.where(columns % (width_all // 2) < rank, value, 0.0)

    def receive(phase, box, level):
        group, slices, width = phases[phase]
        mine = leaf % slices
        folds = folds_of(width)
        rows = rhs // folds
        landed = recvs[phase].at[box]
        pltpu.make_async_copy(landed, landed, p_recv.at[phase, box]).wait()
        total = sends[phase][box, mine].astype(jnp.float32)
        if group <= UNROLL:
            for d in range(group - 1):
                total = total + recvs[phase][box, d].astype(jnp.float32)
        else:
            total = total + jnp.sum(recvs[phase][box].astype(jnp.float32), axis=0)
        total = keep(total, ranks[box, 0, level], mine * width, width)
        if folds > 1:
            total = jnp.concatenate(
                [total[:, f * width : (f + 1) * width] for f in range(folds)], axis=0
            )
        return total.astype(jnp.bfloat16)

    def down_first(level):
        return (width_all >> levels) + 2 * (2 * width_all - (2 * width_all >> level))

    saved = [[None] * boxes for _ in range(levels + 1)]

    def own_terms(level):
        width = width_all >> level
        for box in range(boxes):
            need(down_at[level], box)
            own_sum[level, box] = times(saved[level][box], down, box, down_first(level), width)

    skel_copy.wait()
    ranks_copy.wait()
    for level in range(levels):
        width = width_all >> level
        offset = 2 * width_all - (2 * width_all >> level)
        for box in range(boxes):
            if level == 0:
                block = keep(
                    skel[box, 0].astype(jnp.float32), ranks[box, 0, 0], 0, width_all
                ).astype(jnp.bfloat16)
            else:
                block = receive(level - 1, box, level)
            saved[level][box] = block
            need(up_at[level], box)
            send(level, box, times(block, up, box, offset, width))
        if level == levels - 1:
            own_terms(level)
            if level - 1 > 1:
                own_terms(level - 1)
    phase = levels
    for box in range(boxes):
        block = receive(levels - 1, box, levels)
        need(root_at, box)
        send(phase, box, times(block, down, box, 0, width_all >> levels))
    for level in reversed(range(levels - 2 if levels - 2 > 1 else levels - 1)):
        own_terms(level)
    for level in reversed(range(levels)):
        width = width_all >> level
        for box in range(boxes):
            block = receive(phase, box, level + 1)
            value = own_sum[level, box] + times(
                block, down, box, down_first(level) + width, width
            )
            if level:
                send(phase + 1, box, value)
            else:
                out[box, 0] = keep(value, ranks[box, 0, 0], 0, width_all).astype(out.dtype)
        phase += 1

    for copy in remote:
        copy.wait_send()
    for p, (group, slices, width) in enumerate(phases):
        for box in range(boxes):
            sent = recvs[p].at[box]
            pltpu.make_async_copy(sent, sent, p_send.at[p, box]).wait()


def per_device(dims, leaf_skel, ranks, up_weight, down_weight):
    levels, width_all, boxes, rhs, n_leaf, up_rows, down_rows = dims
    phases = make_phases(levels, width_all)
    chunks = make_chunks(levels, width_all, up_rows, down_rows)[0]
    half = up_weight.shape[-1]

    def piece(width):
        folds = folds_of(width)
        return rhs // folds, folds * width

    sends = [pltpu.VMEM((boxes, s) + piece(w), jnp.bfloat16) for g, s, w in phases]
    recvs = [pltpu.VMEM((boxes, g - 1) + piece(w), jnp.bfloat16) for g, s, w in phases]
    dma = pltpu.SemaphoreType.DMA
    return pl.pallas_call(
        functools.partial(kernel, dims),
        out_shape=jax.ShapeDtypeStruct(leaf_skel.shape, leaf_skel.dtype),
        in_specs=[pl.BlockSpec(memory_space=pltpu.HBM)] * 4,
        out_specs=pl.BlockSpec(memory_space=pltpu.VMEM),
        scratch_shapes=[
            pltpu.VMEM(leaf_skel.shape, jnp.bfloat16),
            pltpu.SMEM(ranks.shape, jnp.int32),
            pltpu.VMEM((2, boxes, up_rows, half), jnp.bfloat16),
            pltpu.VMEM((2, boxes, down_rows, half), jnp.bfloat16),
            pltpu.VMEM((levels, boxes, rhs, width_all), jnp.float32),
        ]
        + sends
        + recvs
        + [
            dma,
            dma,
            dma((len(chunks),)),
            dma((len(chunks),)),
            dma((len(chunks),)),
            dma((len(phases), boxes)),
            dma((len(phases), boxes)),
        ],
        compiler_params=pltpu.CompilerParams(
            collective_id=0, has_side_effects=True, vmem_limit_bytes=60 * 1024 * 1024
        ),
        cost_estimate=pl.CostEstimate(
            flops=4 * boxes * rhs * (up_rows + down_rows) * half * 2,
            bytes_accessed=4 * boxes * (up_rows + down_rows) * half,
            transcendentals=0,
        ),
    )(leaf_skel, ranks, up_weight, down_weight)


def solution(mesh):
    n_leaf, n_rhs = mesh.shape["leaf"], mesh.shape["rhs"]

    def whole(leaf_skel, ranks, up_weight, down_weight):
        dims = (
            ranks.shape[-1] - 1,
            leaf_skel.shape[-1],
            leaf_skel.shape[0],
            leaf_skel.shape[2] // n_rhs,
            n_leaf,
            up_weight.shape[1] // n_leaf,
            down_weight.shape[1] // n_leaf,
        )
        return jax.shard_map(
            functools.partial(per_device, dims),
            mesh=mesh,
            in_specs=(
                P(None, "leaf", "rhs", None),
                P(None, "leaf", None),
                P(None, "leaf", "rhs"),
                P(None, "leaf", "rhs"),
            ),
            out_specs=P(None, "leaf", "rhs", None),
            check_vma=False,
        )(leaf_skel, ranks, up_weight, down_weight)

    return whole
```

```python
import functools

import jax
import jax.numpy as jnp
from jax import lax
from jax.experimental import pallas as pl
from jax.experimental.pallas import tpu as pltpu
from jax.sharding import PartitionSpec as P

MESH = pl.DeviceIdType.MESH
UNROLL = 16


def folds_of(width):
    return 1 if width >= 128 else min(128 // width, 4)


def far_first(group):
    hops = [1, 1, 1, 2]
    count = lambda d: sum(h for bit, h in enumerate(hops) if d >> bit & 1)
    return sorted(range(1, group), key=count, reverse=True)


def make_phases(levels, width_all):
    phases = []
    for level in range(levels):
        group = 2 << level
        phases.append((group, group, width_all // group))
    for level in range(levels, 0, -1):
        group = 1 << level
        slices = 1 if level == 2 else group // 2
        phases.append((group, slices, width_all // slices))
    return phases


def make_chunks(levels, width_all, up_rows, down_rows):
    ups = [(2 * width_all - (2 * width_all >> l), width_all >> l) for l in range(levels)]
    root = width_all >> levels
    downs = [
        (root + 2 * (2 * width_all - (2 * width_all >> l)), 2 * (width_all >> l))
        for l in range(levels)
    ]
    fine = all(o % 16 == 0 and w % 16 == 0 for o, w in ups + downs + [(0, root)])
    if not fine:
        chunks = [(False, None, 0, up_rows), (True, None, 0, down_rows)]
        return chunks, [[0]] * levels, [1], [[1]] * levels
    chunks = [(False, 0) + ups[0], (False, 1) + ups[0]]
    up_at = [[0, 1]]
    for l in range(1, levels):
        up_at.append([len(chunks)])
        chunks.append((False, None) + ups[l])
    root_at = [len(chunks)]
    chunks.append((True, None, 0, root))
    down_at = [None] * levels
    for l in reversed(range(levels)):
        down_at[l] = [len(chunks)]
        chunks.append((True, None) + downs[l])
    return chunks, up_at, root_at, down_at


def kernel(dims, skel_hbm, ranks_hbm, up_hbm, down_hbm, out, *scratch):
    levels, width_all, boxes, rhs, n_leaf, up_rows, down_rows = dims
    phases = make_phases(levels, width_all)
    chunks, up_at, root_at, down_at = make_chunks(levels, width_all, up_rows, down_rows)
    count = len(phases)
    skel, ranks, up, down, own_sum, pair = scratch[:6]
    sends = scratch[6 : 6 + count]
    recvs = scratch[6 + count : 6 + 2 * count]
    skel_sem, ranks_sem, local_sem, w_send, w_recv, p_send, p_recv = scratch[6 + 2 * count : -2]
    pair_send, pair_recv = scratch[-2:]

    leaf = lax.axis_index("leaf")
    core = lax.axis_index("rhs")
    other = 1 - core

    barrier = pltpu.get_barrier_semaphore()
    pl.semaphore_signal(barrier, inc=1, device_id=(leaf, other), device_id_type=MESH)

    for bit in range(levels):
        step = 1 << bit
        target = leaf + step * (1 - 2 * (leaf // step % 2))
        pl.semaphore_signal(barrier, inc=1, device_id=(target, core), device_id_type=MESH)

    def box_rows(chunk):
        is_down, box, first, rows = chunk
        boxes_of = slice(None) if box is None else pl.ds(box, 1)
        source = (down_hbm if is_down else up_hbm).at[boxes_of, pl.ds(first, rows), :]
        target = (down if is_down else up).at[core, boxes_of, pl.ds(first, rows), :]
        return source, target

    def arriving(chunk):
        is_down, box, first, rows = chunk
        boxes_of = slice(None) if box is None else pl.ds(box, 1)
        return (down if is_down else up).at[other, boxes_of, pl.ds(first, rows), :]

    skel_copy = pltpu.make_async_copy(skel_hbm, skel, skel_sem)
    skel_copy.start()
    ranks_copy = pltpu.make_async_copy(ranks_hbm, ranks, ranks_sem)
    ranks_copy.start()
    local = []
    for i, chunk in enumerate(chunks):
        source, target = box_rows(chunk)
        copy = pltpu.make_async_copy(source, target, local_sem.at[i])
        copy.start()
        local.append(copy)

    pl.semaphore_wait(barrier, levels + 1)

    remote = []
    for i, chunk in enumerate(chunks):
        source, target = box_rows(chunk)
        copy = pltpu.make_async_remote_copy(
            src_ref=source,
            dst_ref=target,
            send_sem=w_send.at[i],
            recv_sem=w_recv.at[i],
            device_id=(leaf, other),
            device_id_type=MESH,
        )
        copy.start()
        remote.append(copy)

    width_pair = width_all // 2
    pair_rows = (width_all >> levels) + 2 * width_all + width_pair
    parity = leaf % 2
    part = width_pair // 2
    to_pair = [
        pltpu.make_async_remote_copy(
            src_ref=down_hbm.at[pl.ds(i // 2, 1), pl.ds(pair_rows + i % 2 * part, part), :],
            dst_ref=pair.at[core, pl.ds(i // 2, 1), pl.ds(i % 2 * part, part), :],
            send_sem=pair_send.at[1 + i],
            recv_sem=pair_recv.at[1 + i],
            device_id=(leaf + 1 - 2 * parity, core),
            device_id_type=MESH,
        )
        for i in range(2 * boxes)
    ]
    to_core = pltpu.make_async_remote_copy(
        src_ref=pair.at[core],
        dst_ref=pair.at[core],
        send_sem=pair_send.at[0],
        recv_sem=pair_recv.at[0],
        device_id=(leaf, other),
        device_id_type=MESH,
    )

    ready = set()

    def need(indices, box):
        for i in indices:
            if i in ready or chunks[i][1] not in (None, box):
                continue
            ready.add(i)
            local[i].wait()
            landed = arriving(chunks[i])
            pltpu.make_async_copy(landed, landed, w_recv.at[i]).wait()

    def times(block, weights, box, first, rows):
        return jnp.concatenate(
            [
                jnp.dot(
                    block,
                    weights[half, box, first : first + rows, :],
                    preferred_element_type=jnp.float32,
                )
                for half in range(2)
            ],
            axis=1,
        )

    def send(phase, box, value):
        group, slices, width = phases[phase]
        member = leaf % group
        base = leaf - member
        folds = folds_of(width)
        rows = rhs // folds
        value = value.astype(jnp.bfloat16)
        for k in range(slices):
            piece = value[:, k * width : (k + 1) * width]
            if folds > 1:
                piece = jnp.concatenate(
                    [piece[f * rows : (f + 1) * rows] for f in range(folds)], axis=1
                )
            sends[phase][box, k] = piece

        def one(d):
            there = member
            for bit in range(group.bit_length() - 1):
                step = 1 << bit
                there = there + step * (d // step % 2) * (1 - 2 * (member // step % 2))
            pltpu.make_async_remote_copy(
                src_ref=sends[phase].at[box, there % slices],
                dst_ref=recvs[phase].at[box, d - 1],
                send_sem=p_send.at[phase, box],
                recv_sem=p_recv.at[phase, box],
                device_id=(base + there, core),
                device_id_type=MESH,
            ).start()

        if group <= UNROLL:
            for d in far_first(group):
                one(d)
        else:
            pl.loop(1, group)(one)

    def keep(value, rank, first_column, width):
        columns = lax.broadcasted_iota(jnp.int32, value.shape, 1) % width + first_column
        return jnp.where(columns % (width_all // 2) < rank, value, 0.0)

    def gather(phase, box):
        group, slices, width = phases[phase]
        mine = leaf % slices
        landed = recvs[phase].at[box]
        pltpu.make_async_copy(landed, landed, p_recv.at[phase, box]).wait()
        total = sends[phase][box, mine].astype(jnp.float32)
        if group <= UNROLL:
            for d in range(group - 1):
                total = total + recvs[phase][box, d].astype(jnp.float32)
        else:
            total = total + jnp.sum(recvs[phase][box].astype(jnp.float32), axis=0)
        return total

    def receive(phase, box, level):
        group, slices, width = phases[phase]
        mine = leaf % slices
        folds = folds_of(width)
        total = keep(gather(phase, box), ranks[box, 0, level], mine * width, width)
        if folds > 1:
            total = jnp.concatenate(
                [total[:, f * width : (f + 1) * width] for f in range(folds)], axis=0
            )
        return total.astype(jnp.bfloat16)

    def down_first(level):
        return (width_all >> levels) + 2 * (2 * width_all - (2 * width_all >> level))

    saved = [[None] * boxes for _ in range(levels + 1)]

    def own_terms(level):
        width = width_all >> level
        for box in range(boxes):
            need(down_at[level], box)
            terms = times(saved[level][box], down, box, down_first(level), width)
            if level == 1:
                send(count - 1, box, terms)
            else:
                own_sum[level, box] = terms

    skel_copy.wait()
    ranks_copy.wait()
    for level in range(levels):
        width = width_all >> level
        offset = 2 * width_all - (2 * width_all >> level)
        for box in range(boxes):
            if level == 0:
                block = keep(
                    skel[box, 0].astype(jnp.float32), ranks[box, 0, 0], 0, width_all
                ).astype(jnp.bfloat16)
            else:
                block = receive(level - 1, box, level)
            saved[level][box] = block
            need(up_at[level], box)
            send(level, box, times(block, up, box, offset, width))
        for copy in to_pair[level:] if level == levels - 1 else to_pair[level : level + 1]:
            copy.start()
        if level == levels - 1:
            own_terms(level)
            if level - 1 > 1:
                own_terms(level - 1)
    phase = levels
    for box in range(boxes):
        block = receive(levels - 1, box, levels)
        need(root_at, box)
        send(phase, box, times(block, down, box, 0, width_all >> levels))
    for level in reversed(range(levels - 2 if levels - 2 > 1 else levels - 1)):
        own_terms(level)
    for copy in to_pair:
        copy.wait_recv()
    to_core.start()
    for level in reversed(range(levels)):
        width = width_all >> level
        if level == 1:
            phase += 1
            continue
        for box in range(boxes):
            if level:
                block = receive(phase, box, level + 1)
            else:
                above = receive(phase - 1, box, 2)
                if box == 0:
                    arrived = pair.at[other]
                    pltpu.make_async_copy(arrived, arrived, pair_recv.at[0]).wait()
                low, high = above[:, :width_pair], above[:, width_pair:]
                mine = jnp.where(parity == 0, low, high)
                theirs = jnp.where(parity == 0, high, low)
                total = gather(phase, box)
                total = total + times(mine, down, box, pair_rows, width_pair)
                total = total + times(theirs, pair, box, 0, width_pair)
                block = keep(total, ranks[box, 0, 1], 0, width_all).astype(jnp.bfloat16)
            value = own_sum[level, box] + times(
                block, down, box, down_first(level) + width, width
            )
            if level:
                send(phase + 1, box, value)
            else:
                out[box, 0] = keep(value, ranks[box, 0, 0], 0, width_all).astype(out.dtype)
        phase += 1

    for copy in remote + to_pair + [to_core]:
        copy.wait_send()
    for p, (group, slices, width) in enumerate(phases):
        for box in range(boxes):
            sent = recvs[p].at[box]
            pltpu.make_async_copy(sent, sent, p_send.at[p, box]).wait()


def per_device(dims, leaf_skel, ranks, up_weight, down_weight):
    levels, width_all, boxes, rhs, n_leaf, up_rows, down_rows = dims
    phases = make_phases(levels, width_all)
    chunks = make_chunks(levels, width_all, up_rows, down_rows)[0]
    half = up_weight.shape[-1]

    def piece(width):
        folds = folds_of(width)
        return rhs // folds, folds * width

    sends = [pltpu.VMEM((boxes, s) + piece(w), jnp.bfloat16) for g, s, w in phases]
    recvs = [pltpu.VMEM((boxes, g - 1) + piece(w), jnp.bfloat16) for g, s, w in phases]
    dma = pltpu.SemaphoreType.DMA
    return pl.pallas_call(
        functools.partial(kernel, dims),
        out_shape=jax.ShapeDtypeStruct(leaf_skel.shape, leaf_skel.dtype),
        in_specs=[pl.BlockSpec(memory_space=pltpu.HBM)] * 4,
        out_specs=pl.BlockSpec(memory_space=pltpu.VMEM),
        scratch_shapes=[
            pltpu.VMEM(leaf_skel.shape, jnp.bfloat16),
            pltpu.SMEM(ranks.shape, jnp.int32),
            pltpu.VMEM((2, boxes, up_rows, half), jnp.bfloat16),
            pltpu.VMEM((2, boxes, down_rows, half), jnp.bfloat16),
            pltpu.VMEM((levels, boxes, rhs, width_all), jnp.float32),
            pltpu.VMEM((2, boxes, width_all // 2, half), jnp.bfloat16),
        ]
        + sends
        + recvs
        + [
            dma,
            dma,
            dma((len(chunks),)),
            dma((len(chunks),)),
            dma((len(chunks),)),
            dma((len(phases), boxes)),
            dma((len(phases), boxes)),
            dma((1 + 2 * boxes,)),
            dma((1 + 2 * boxes,)),
        ],
        compiler_params=pltpu.CompilerParams(
            collective_id=0, has_side_effects=True, vmem_limit_bytes=60 * 1024 * 1024
        ),
        cost_estimate=pl.CostEstimate(
            flops=4 * boxes * rhs * (up_rows + down_rows) * half * 2,
            bytes_accessed=4 * boxes * (up_rows + down_rows) * half,
            transcendentals=0,
        ),
    )(leaf_skel, ranks, up_weight, down_weight)


def solution(mesh):
    n_leaf, n_rhs = mesh.shape["leaf"], mesh.shape["rhs"]

    def whole(leaf_skel, ranks, up_weight, down_weight):
        dims = (
            ranks.shape[-1] - 1,
            leaf_skel.shape[-1],
            leaf_skel.shape[0],
            leaf_skel.shape[2] // n_rhs,
            n_leaf,
            up_weight.shape[1] // n_leaf,
            down_weight.shape[1] // n_leaf,
        )
        return jax.shard_map(
            functools.partial(per_device, dims),
            mesh=mesh,
            in_specs=(
                P(None, "leaf", "rhs", None),
                P(None, "leaf", None),
                P(None, "leaf", "rhs"),
                P(None, "leaf", "rhs"),
            ),
            out_specs=P(None, "leaf", "rhs", None),
            check_vma=False,
        )(leaf_skel, ranks, up_weight, down_weight)

    return whole
```
